32 devices in a mesh: row: 8 (over y, x, core), col: 4 (over z).
Axes of the slice: x: 2, y: 2, z: 4, core: 2. Of those that a mesh axis runs over, the one named last changes fastest.
Arguments:
- sensitivity: float32 [16384, 16384], P('row', 'col'), as said below
- injection: float32 [16384, 1024], P('col', 'row'), may hold values from -6 to 6
- dispatch_now: float32 [16384, 1024], P('row', 'col'), may hold values from -3 to 3
- limit_class: int32 [16384], P('row'), may hold values from 0 to 15
- box_table: float32 [16], replicated, may hold values from 0.3 to 1.5
- owner_index: int32 [16384, 1], P('row'), may hold values from 0 to 7; in each aligned block of 2048 rows (0 to 2047, 2048 to 4095, ...) at most 768 rows name the same one
- member_slot: int32 [16384], P('row'), may hold values from 0 to 127
- agg_limit: float32 [1024], P('row'), may hold values from 0.5 to 4
Outputs:
- dispatch: float32 [16384, 1024], P('row', 'col')
- aggregate: float32 [1024, 1024], P('row', 'col')
The draws below stay inside these ranges and needn't reach their ends.
Inputs may be any that keep to these rules, and one draw needn't show every extreme that they name: `sensitivity`: symmetric. `owner_index`: in each aligned block of 2048 inverters (those of one index of row) at most 768 have the same owner, and some owner has exactly 768 in some block.
All inputs are finite; a program needn't handle non-finite values.
Results may differ from the reference program's by a relative error of at most 0.000088.
Values sent between devices are 32-bit elements; how exact they have to be, the bound alone decides.
A program may use at most 128 MiB of HBM per device.

```python
import math
import jax
import jax.numpy as jnp
import numpy as np
from jax import lax

N = 16384
S = 1024
AGG_DEV = 128
LIMITS = 16
ROWS_DEV = 2048
OWNERS = 8
CAP = 768
AGGS = 1024


def draw_sensitivity(key, part):
    key_base = jax.random.fold_in(key, 11)
    key_diag = jax.random.fold_in(key, 12)
    base_draw = jax.random.normal(key_base, (N, N), jnp.float32)
    off_part = (base_draw + base_draw.T) * 0.5 ** 0.5 / math.sqrt(N)
    diagonal_part = jax.random.uniform(key_diag, (N,), jnp.float32, 1.0, 2.0)
    on_diagonal = jnp.arange(N)[:, None] == jnp.arange(N)[None, :]
    return jnp.where(on_diagonal, diagonal_part[:, None], off_part)


def place_ends(entries, key, smallest, high):
    index_at = [jax.random.randint(jax.random.fold_in(key, axis), (), 0, length) for axis, length in enumerate(entries.shape)]
    main_axis = entries.shape.index(max(entries.shape))
    neighbour = index_at[:main_axis] + [(index_at[main_axis] + 1) % entries.shape[main_axis]] + index_at[main_axis + 1:]
    return entries.at[tuple(index_at)].set(smallest).at[tuple(neighbour)].set(high)


def shard_levels(stream_key, dims, split, smallest, largest):
    loudness = 1.0
    for position, shards_of in split:
        steps = jax.random.uniform(jax.random.fold_in(jax.random.fold_in(stream_key, 6), position), (shards_of,), jnp.float32, smallest / len(split), largest / len(split))
        loudness = loudness * jnp.repeat(jnp.exp(steps), dims[position] // shards_of).reshape((-1,) + (1,) * (len(dims) - 1 - position))
    return loudness


def assign_block(key, own, number, rows, number_of, top, bound, lean):
    order = jax.random.permutation(key, number_of)
    packed, usual = portions_of(number_of, rows * top, bound, lean, True), portions_of(number_of, rows * top, bound, lean, False)
    places = jnp.arange(number_of)

    def named(tallies, rotation):
        used = int((tallies > 0).sum())
        fixed = max(1, used // 4)
        moved = fixed + (places - fixed + rotation * (used - fixed)) % max(1, number_of - fixed)
        return jnp.zeros((number_of,), jnp.int32).at[order[jnp.where(places < fixed, places, moved)]].set(jnp.asarray(tallies, jnp.int32))

    tallies = jnp.where(number % 4 == 0, named(packed, number // 4), named(usual, number - number // 4 - 1))
    mixed = jax.random.permutation(jax.random.fold_in(own, 3), number_of)
    source_of, sink = mixed[0:number_of // 2 * 2:2], mixed[1:number_of // 2 * 2:2]
    room = jnp.minimum(tallies[source_of] - 1, bound - tallies[sink]) // 2
    room = jnp.where((source_of == order[0]) | (sink == order[0]) | (tallies[sink] == 0), 0, jnp.maximum(room, 0))
    moved = jax.random.randint(jax.random.fold_in(own, 4), (number_of // 2,), 0, 1 << 20) % (room + 1)
    tallies = tallies.at[source_of].add(-moved).at[sink].add(moved)
    items = jnp.searchsorted(jnp.cumsum(tallies), jnp.arange(rows * top), side="right").astype(jnp.int32)
    table = items.reshape(top, rows).T
    table = table[jax.random.permutation(jax.random.fold_in(own, 1), rows)]
    rotation = jax.random.randint(jax.random.fold_in(own, 2), (rows, 1), 0, top)
    return jnp.take_along_axis(table, (jnp.arange(top)[None, :] + rotation) % top, axis=1)


def portions_of(count, total, most, slope, full):
    weights = [(1 << 20) // math.isqrt(standing ** slope) + 1 for standing in range(1, count + 1)]
    largest = most if full else min(most, max(-(-total // count), total * weights[0] // sum(weights)))
    least = 1 if total - largest >= count - 1 else 0
    given, surplus = [largest] + [least] * (count - 1), total - largest - least * (count - 1)
    while surplus > 0:
        free = [i for i in range(1, count) if given[i] < largest] or [i for i in range(1, count) if given[i] < most]
        pool, left = sum([weights[i] for i in free]), surplus
        for i in free:
            extra = min(most - given[i], max(1, left * weights[i] // pool), surplus)
            given[i] = given[i] + extra
            surplus = surplus - extra
    return np.array(given)


def noise(own_key, extent, deviation, limit, pieces=(), held_as=jnp.bfloat16):
    loudness = shard_levels(own_key, extent, pieces, -0.22, 0.18) if pieces else 1.0
    entries = jax.random.normal(own_key, extent, jnp.float32) * deviation * loudness
    return jnp.minimum(jnp.maximum(entries, -limit), limit).astype(held_as)


def setup_inputs(seed: int = 0) -> dict:
    key_of = jax.random.split(jax.random.key(seed), 9)
    sensitivity = draw_sensitivity(jax.random.fold_in(key_of[8], 71), 0)
    injection = noise(key_of[1], (N, S), 1.0, 6.0, ((0, 4), (1, 8)), jnp.float32)
    dispatch_now = noise(key_of[2], (N, S), 0.5, 3.0, ((0, 8), (1, 4)), jnp.float32)
    limit_class = place_ends(jax.random.randint(key_of[3], (N,), 0, LIMITS), jax.random.fold_in(key_of[3], 1), 0, LIMITS - 1).astype(jnp.int32)
    box_table = jnp.clip(jnp.exp(jax.random.uniform(key_of[4], (LIMITS,), jnp.float32, math.log(0.3), math.log(1.5))), 0.3, 1.5)
    owner_index_keys = jax.random.split(jax.random.fold_in(key_of[5], 1), N // ROWS_DEV)
    owner_index_turns = jax.random.permutation(jax.random.fold_in(key_of[5], 3), N // ROWS_DEV)
    owner_index = jax.vmap(lambda own, number: assign_block(jax.random.fold_in(key_of[5], 2), own, number, ROWS_DEV, OWNERS, 1, CAP, 2))(owner_index_keys, owner_index_turns).reshape((N, 1))
    member_slot = place_ends(jax.random.randint(key_of[6], (N,), 0, AGG_DEV), jax.random.fold_in(key_of[6], 1), 0, AGG_DEV - 1).astype(jnp.int32)
    agg_limit = jnp.clip(jnp.exp(math.log(4.0) - 2.0794415 * jax.random.uniform(key_of[7], (AGGS,), jnp.float32) ** shard_levels(key_of[7], (AGGS,), ((0, 8),), -0.2, 0.2)), 0.5, 4.0)
    return dict(sensitivity=sensitivity, injection=injection, dispatch_now=dispatch_now, limit_class=limit_class, box_table=box_table, owner_index=owner_index, member_slot=member_slot, agg_limit=agg_limit)


step_size = 0.1


def reference(sensitivity, injection, dispatch_now, limit_class, box_table, owner_index, member_slot, agg_limit):
    gradient = 2.0 * jnp.dot(sensitivity, injection, precision=lax.Precision.HIGHEST, preferred_element_type=jnp.float32)
    box_bound = box_table[limit_class][:, None]
    stepped = jnp.clip(dispatch_now - step_size * gradient, -box_bound, box_bound)
    agg_id = (owner_index[:, 0] * AGG_DEV + member_slot).astype(jnp.int32)
    total = jax.ops.segment_sum(stepped, agg_id, num_segments=AGGS)
    limit_col = agg_limit[:, None]
    factor = limit_col / jnp.maximum(jnp.abs(total), limit_col)
    aggregate = total * factor
    dispatch = stepped * factor[agg_id]
    return dispatch, aggregate
```

```python
import jax
import jax.numpy as jnp
from jax import lax
from jax.sharding import PartitionSpec as P

step_size = 0.1


chunks = 4


def rounded(x):
    return lax.reduce_precision(x, exponent_bits=8, mantissa_bits=7)


def split3(x):
    hi = rounded(x)
    rest = x - hi
    mid = rounded(rest)
    return tuple(part.astype(jnp.bfloat16) for part in (hi, mid, rest - mid))


def body(
    sensitivity,
    injection,
    dispatch_now,
    limit_class,
    box_table,
    owner_index,
    member_slot,
    agg_limit,
):
    owners = lax.axis_size("row")
    agg_dev = agg_limit.shape[0]
    row_count = sensitivity.shape[0]
    injection_t = injection.T
    width = injection_t.shape[0] // chunks
    group = owners // lax.axis_size("col")
    gradients = []
    for chunk in range(chunks):
        part = injection_t[chunk * width : (chunk + 1) * width]
        part = lax.all_gather(part, "row", axis=0, tiled=True)
        partial_value = lax.dot_general(
            part,
            sensitivity,
            (((1,), (1,)), ((), ())),
            precision=lax.Precision.HIGH,
            preferred_element_type=jnp.float32,
        )
        summed = lax.psum_scatter(partial_value, "col", scatter_dimension=0, tiled=True)
        gradients.append(summed.reshape(group, width, row_count))
    gradient = 2.0 * jnp.concatenate(gradients, axis=1).reshape(-1, row_count).T
    classes = jnp.arange(box_table.shape[0], dtype=jnp.int32)
    box_bound = jnp.sum(
        jnp.where(limit_class[:, None] == classes[None, :], box_table[None, :], 0.0), axis=1
    )[:, None]
    stepped = jnp.clip(dispatch_now - step_size * gradient, -box_bound, box_bound)
    agg_id = owner_index[:, 0] * agg_dev + member_slot
    aggs = owners * agg_dev
    selector = (agg_id[None, :] == jnp.arange(aggs, dtype=jnp.int32)[:, None]).astype(jnp.bfloat16)

    def pick(left, parts, dims):
        return sum(
            lax.dot_general(left, part, (dims, ((), ())), preferred_element_type=jnp.float32)
            for part in parts
        )

    local = pick(selector, split3(stepped), ((1,), (0,)))
    total = lax.psum_scatter(local, "row", scatter_dimension=0, tiled=True)
    limit_col = agg_limit[:, None]
    factor = limit_col / jnp.maximum(jnp.abs(total), limit_col)
    aggregate = total * factor
    all_factor = lax.all_gather(factor, "row", axis=0, tiled=True)
    own_factor = pick(selector, split3(all_factor), ((0,), (0,)))
    return (stepped * own_factor, aggregate)


def solution(mesh):
    placed = (
        P("row", "col"),
        P("col", "row"),
        P("row", "col"),
        P("row"),
        P(),
        P("row", None),
        P("row"),
        P("row"),
    )
    return jax.shard_map(
        body,
        mesh=mesh,
        in_specs=placed,
        out_specs=(P("row", "col"), P("row", "col")),
        check_vma=False,
    )
```

```python
import jax
import jax.numpy as jnp
from jax import lax
from jax.sharding import PartitionSpec as P

step_size = 0.1


portions = (2, 3, 5, 6)


def gather_row(part, after):
    count = lax.axis_size("row")
    me = lax.axis_index("row")

    def swap(value, distance):
        return lax.ppermute(value, "row", [(r, r ^ distance) for r in range(count)])

    if after is not None:
        part, _ = lax.optimization_barrier((part, after))
    own = {0: part}
    for distance in range(2, count, 2):
        own[distance] = swap(part, distance)
    parts = dict(own)
    for distance, value in own.items():
        parts[distance ^ 1] = swap(value, 1)
    whole = jnp.zeros((count,) + part.shape, part.dtype)
    for distance, value in parts.items():
        whole = lax.dynamic_update_index_in_dim(whole, value, me ^ distance, 0)
    return whole.reshape((-1,) + part.shape[1:]), list(own.values())[1:]


def rounded(x):
    return lax.reduce_precision(x, exponent_bits=8, mantissa_bits=7)


def split3(x):
    hi = rounded(x)
    rest = x - hi
    mid = rounded(rest)
    return tuple(part.astype(jnp.bfloat16) for part in (hi, mid, rest - mid))


def body(
    sensitivity,
    injection,
    dispatch_now,
    limit_class,
    box_table,
    owner_index,
    member_slot,
    agg_limit,
):
    owners = lax.axis_size("row")
    agg_dev = agg_limit.shape[0]
    row_count = sensitivity.shape[0]
    injection_t = injection.T
    group = owners // lax.axis_size("col")
    gradients = []
    start, after = 0, None
    for portion in portions:
        width = injection_t.shape[0] * portion // 16
        part, after = gather_row(injection_t[start : start + width], after)
        start += width
        partial_value = lax.dot_general(
            part,
            sensitivity,
            (((1,), (1,)), ((), ())),
            precision=lax.Precision.HIGH,
            preferred_element_type=jnp.float32,
        )
        summed = lax.psum_scatter(partial_value, "col", scatter_dimension=0, tiled=True)
        gradients.append(summed.reshape(group, width, row_count))
    gradient = 2.0 * jnp.concatenate(gradients, axis=1).reshape(-1, row_count).T
    classes = jnp.arange(box_table.shape[0], dtype=jnp.int32)
    box_bound = jnp.sum(
        jnp.where(limit_class[:, None] == classes[None, :], box_table[None, :], 0.0), axis=1
    )[:, None]
    stepped = jnp.clip(dispatch_now - step_size * gradient, -box_bound, box_bound)
    agg_id = owner_index[:, 0] * agg_dev + member_slot
    aggs = owners * agg_dev
    selector = (agg_id[None, :] == jnp.arange(aggs, dtype=jnp.int32)[:, None]).astype(jnp.bfloat16)

    def pick(left, parts, dims):
        return sum(
            lax.dot_general(left, part, (dims, ((), ())), preferred_element_type=jnp.float32)
            for part in parts
        )

    local = pick(selector, split3(stepped), ((1,), (0,)))
    local = local.reshape(owners, agg_dev, -1)
    total = jnp.sum(lax.all_to_all(local, "row", 0, 0, tiled=True), axis=0)
    limit_col = agg_limit[:, None]
    factor = limit_col / jnp.maximum(jnp.abs(total), limit_col)
    aggregate = total * factor
    copies = jnp.broadcast_to(factor[None], (owners,) + factor.shape)
    all_factor = lax.all_to_all(copies, "row", 0, 0, tiled=True).reshape(aggs, -1)
    own_factor = pick(selector, split3(all_factor), ((0,), (0,)))
    return (stepped * own_factor, aggregate)


def solution(mesh):
    placed = (
        P("row", "col"),
        P("col", "row"),
        P("row", "col"),
        P("row"),
        P(),
        P("row", None),
        P("row"),
        P("row"),
    )
    return jax.shard_map(
        body,
        mesh=mesh,
        in_specs=placed,
        out_specs=(P("row", "col"), P("row", "col")),
        check_vma=False,
    )
```

```python
import jax
import jax.numpy as jnp
from jax import lax
from jax.sharding import PartitionSpec as P

step_size = 0.1


portions = (2, 3, 5, 6)


def gather_row(part, after):
    count = lax.axis_size("row")
    me = lax.axis_index("row")

    def swap(value, distance):
        return lax.ppermute(value, "row", [(r, r ^ distance) for r in range(count)])

    if after is not None:
        part, _ = lax.optimization_barrier((part, after))
    own = {0: part}
    for distance in range(2, count, 2):
        own[distance] = swap(part, distance)
    parts = dict(own)
    for distance, value in own.items():
        parts[distance ^ 1] = swap(value, 1)
    whole = jnp.zeros((count,) + part.shape, part.dtype)
    for distance, value in parts.items():
        whole = lax.dynamic_update_index_in_dim(whole, value, me ^ distance, 0)
    return whole.reshape((-1,) + part.shape[1:]), list(own.values())[1:]


def rounded(x):
    return lax.reduce_precision(x, exponent_bits=8, mantissa_bits=7)


def split2(x):
    hi = rounded(x)
    return hi.astype(jnp.bfloat16), (x - hi).astype(jnp.bfloat16)


def split3(x):
    hi = rounded(x)
    rest = x - hi
    mid = rounded(rest)
    return tuple(part.astype(jnp.bfloat16) for part in (hi, mid, rest - mid))


def across(left, right):
    return lax.dot_general(
        left, right, (((1,), (1,)), ((), ())), preferred_element_type=jnp.float32
    )


def scatter_row(blocks):
    count = lax.axis_size("row")
    me = lax.axis_index("row")
    core = me % 2
    pairs = blocks.reshape((count // 2, 2) + blocks.shape[1:])
    other = lax.dynamic_index_in_dim(pairs, 1 - core, 1, keepdims=False)
    mine = lax.dynamic_index_in_dim(pairs, core, 1, keepdims=False)
    mine = mine + lax.ppermute(other, "row", [(r, r ^ 1) for r in range(count)])
    total = lax.dynamic_index_in_dim(mine, me // 2, 0, keepdims=False)
    for distance in range(2, count, 2):
        block = lax.dynamic_index_in_dim(mine, (me ^ distance) // 2, 0, keepdims=False)
        total = total + lax.ppermute(block, "row", [(r, r ^ distance) for r in range(count)])
    return total


def body(
    sensitivity,
    injection,
    dispatch_now,
    limit_class,
    box_table,
    owner_index,
    member_slot,
    agg_limit,
):
    owners = lax.axis_size("row")
    agg_dev = agg_limit.shape[0]
    row_count = sensitivity.shape[0]
    sensitivity_hi, sensitivity_lo = split2(sensitivity)
    injection_t = injection.T
    group = owners // lax.axis_size("col")
    gradients = []
    start, after = 0, None
    for portion in portions:
        width = injection_t.shape[0] * portion // 16
        part, after = gather_row(injection_t[start : start + width], after)
        start += width
        part_hi, part_lo = split2(part)
        partial_value = (
            across(part_lo, sensitivity_hi)
            + across(part_hi, sensitivity_lo)
            + across(part_hi, sensitivity_hi)
        )
        summed = lax.psum_scatter(partial_value, "col", scatter_dimension=0, tiled=True)
        gradients.append(summed.reshape(group, width, row_count))
    gradient = 2.0 * jnp.concatenate(gradients, axis=1).reshape(-1, row_count).T
    classes = jnp.arange(box_table.shape[0], dtype=jnp.int32)
    box_bound = jnp.sum(
        jnp.where(limit_class[:, None] == classes[None, :], box_table[None, :], 0.0), axis=1
    )[:, None]
    stepped = jnp.clip(dispatch_now - step_size * gradient, -box_bound, box_bound)
    agg_id = owner_index[:, 0] * agg_dev + member_slot
    aggs = owners * agg_dev
    selector = (agg_id[None, :] == jnp.arange(aggs, dtype=jnp.int32)[:, None]).astype(jnp.bfloat16)

    def pick(left, parts, dims):
        return sum(
            lax.dot_general(left, part, (dims, ((), ())), preferred_element_type=jnp.float32)
            for part in parts
        )

    local = pick(selector, split3(stepped), ((1,), (0,)))
    local = local.reshape(owners, agg_dev, -1)
    total = scatter_row(local)
    limit_col = agg_limit[:, None]
    factor = limit_col / jnp.maximum(jnp.abs(total), limit_col)
    aggregate = total * factor
    all_factor, _ = gather_row(factor, None)
    own_factor = pick(selector, split3(all_factor), ((0,), (0,)))
    return (stepped * own_factor, aggregate)


def solution(mesh):
    placed = (
        P("row", "col"),
        P("col", "row"),
        P("row", "col"),
        P("row"),
        P(),
        P("row", None),
        P("row"),
        P("row"),
    )
    return jax.shard_map(
        body,
        mesh=mesh,
        in_specs=placed,
        out_specs=(P("row", "col"), P("row", "col")),
        check_vma=False,
    )
```
